32 devices in a mesh: row: 4 (over z), col: 4 (over y, core), depth: 2 (over x).
Axes of the slice: x: 2, y: 2, z: 4, core: 2. Of those that a mesh axis runs over, the one named last changes fastest.
Arguments:
- layer_input: bfloat16 [384, 6144], P(('depth', 'col'), 'row'), may hold values from -6 to 6
- w_in: bfloat16 [6144, 24576], P('row', 'col'), may hold values from -0.078125 to 0.078125
- w_out: bfloat16 [24576, 6144], P('col', 'row'), may hold values from -0.0390625 to 0.0390625
- out_grad: bfloat16 [384, 6144], P(('depth', 'col'), 'row'), may hold values from -1.3515625 to 1.3515625
- drop_seed: int32 [1], replicated, may hold values from 0 to 1073741823
- drop_step: int32 [1], replicated, may hold values from 0 to 999999
Outputs:
- input_grad: float32 [384, 6144], P(('depth', 'col'), 'row')
- w_in_grad: float32 [6144, 24576], P('row', ('col', 'depth'))
- w_out_grad: float32 [24576, 6144], P('col', ('row', 'depth'))
The draws below stay inside these ranges and needn't reach their ends.
All inputs are finite; a program needn't handle non-finite values.
Results may differ from the reference program's by a relative error of at most 0.0041.
Values may be sent and summed in bfloat16 or wider, within the bound.
No kernel may reach another device: no remote copies, remote signals or barrier semaphores. Data moves between devices by JAX's collectives and lax.ppermute only.
A program may use at most 128 MiB of HBM per device.

```python
import math
import jax
import jax.numpy as jnp
from jax import lax

D = 6144
FF = 24576
TOKENS = 384


def levels(rng, extent, pieces, smallest, largest):
    gain, own = 1.0, jax.random.fold_in(rng, 6)
    for axis_at, blocks in pieces:
        steps = jnp.exp(jax.random.uniform(jax.random.fold_in(own, axis_at), (blocks,), jnp.float32, smallest / len(pieces), largest / len(pieces)))
        gain = gain * jnp.repeat(steps, extent[axis_at] // blocks).reshape([-1 if axis == axis_at else 1 for axis in range(len(extent))])
    return gain


def noise(own_key, extent, deviation, reach, cuts=(), held_as=jnp.bfloat16):
    result = deviation * jax.random.normal(own_key, extent, jnp.float32)
    if cuts:
        result = result * levels(own_key, extent, cuts, -0.22, 0.18)
    return jnp.clip(result, -reach, reach).astype(held_as)


def setup_inputs(seed: int = 0) -> dict:
    splits = jax.random.split(jax.random.key(seed), 7)
    return {
        "layer_input": noise(splits[0], (TOKENS, D), 1.0, 6.0, ((0, 8), (1, 4))),
        "w_in": noise(splits[1], (D, FF), D ** -0.5, 0.078125, ((0, 4), (1, 4))),
        "w_out": noise(splits[2], (FF, D), FF ** -0.5, 0.0390625, ((0, 4), (1, 4))),
        "out_grad": noise(splits[3], (TOKENS, D), (TOKENS ** -0.25), 1.3515625, ((0, 8), (1, 4))),
        "drop_seed": jax.random.randint(splits[4], (1,), 0, 1073741824).astype(jnp.int32),
        "drop_step": jax.random.randint(splits[5], (1,), 0, 1000000).astype(jnp.int32),
    }


keep_scale = 1.0 / 0.9
gelu_coef = math.sqrt(2.0 / math.pi)

def mix_bits(word_bits):
    word_bits = word_bits ^ lax.shift_right_logical(word_bits, jnp.int32(16))
    word_bits = word_bits * jnp.int32(2146121005)
    word_bits = word_bits ^ lax.shift_right_logical(word_bits, jnp.int32(15))
    word_bits = word_bits * jnp.int32(-2073254261)
    word_bits = word_bits ^ lax.shift_right_logical(word_bits, jnp.int32(16))
    return word_bits

def keep_mask(drop_seed, drop_step, row_start, col_start, row_count, col_count, row_length):
    stream_key = mix_bits(mix_bits(drop_step[0] + jnp.int32(1013904223)) ^ drop_seed[0])
    row_ids = jnp.arange(row_count, dtype=jnp.int32) + row_start
    col_ids = jnp.arange(col_count, dtype=jnp.int32) + col_start
    flat_index = row_ids[:, None] * jnp.int32(row_length) + col_ids[None, :]
    hashed = mix_bits(flat_index ^ stream_key)
    return hashed & jnp.int32(16777215) < jnp.int32(15099494)

def gelu_parts(hidden_pre):
    inner_arg = gelu_coef * (hidden_pre + 0.044715 * hidden_pre * hidden_pre * hidden_pre)
    tanh_val = jnp.tanh(inner_arg)
    act_full = 0.5 * hidden_pre * (1.0 + tanh_val)
    gelu_slope = 0.5 * (1.0 + tanh_val) + 0.5 * hidden_pre * (1.0 - tanh_val * tanh_val) * gelu_coef * (1.0 + 3.0 * 0.044715 * hidden_pre * hidden_pre)
    return (act_full, gelu_slope)

def reference(layer_input, w_in, w_out, out_grad, drop_seed, drop_step):
    hidden_pre = jnp.dot(layer_input, w_in, preferred_element_type=jnp.float32)
    act_full, gelu_slope = gelu_parts(hidden_pre)
    hidden_act = act_full.astype(jnp.bfloat16)
    keep_flags = keep_mask(drop_seed, drop_step, jnp.int32(0), jnp.int32(0), TOKENS, D, D)
    scaled = jnp.where(keep_flags, out_grad.astype(jnp.float32) * keep_scale, jnp.zeros((), jnp.float32)).astype(jnp.bfloat16)
    act_grad = lax.dot_general(scaled, w_out, (((1,), (1,)), ((), ())), preferred_element_type=jnp.float32)
    pre_grad = (act_grad * gelu_slope).astype(jnp.bfloat16)
    w_out_grad = lax.dot_general(hidden_act, scaled, (((0,), (0,)), ((), ())), preferred_element_type=jnp.float32)
    w_in_grad = lax.dot_general(layer_input, pre_grad, (((0,), (0,)), ((), ())), preferred_element_type=jnp.float32)
    input_grad = lax.dot_general(pre_grad, w_in, (((1,), (1,)), ((), ())), preferred_element_type=jnp.float32)
    return (input_grad, w_in_grad, w_out_grad)
```

```python
import functools
import math

import jax
import jax.numpy as jnp
from jax import lax
from jax.experimental import pallas as pl
from jax.experimental.pallas import tpu as pltpu
from jax.sharding import PartitionSpec as P

D = 6144
CHUNKS = 8
VMEM_LIMIT = 40 * 1024 * 1024

keep_scale = 1.0 / 0.9
gelu_coef = math.sqrt(2.0 / math.pi)

F32, BF16 = jnp.float32, jnp.bfloat16


def mix_bits(word_bits):
    word_bits = word_bits ^ lax.shift_right_logical(word_bits, jnp.int32(16))
    word_bits = word_bits * jnp.int32(2146121005)
    word_bits = word_bits ^ lax.shift_right_logical(word_bits, jnp.int32(15))
    word_bits = word_bits * jnp.int32(-2073254261)
    word_bits = word_bits ^ lax.shift_right_logical(word_bits, jnp.int32(16))
    return word_bits


def keep_mask(drop_seed, drop_step, row_start, col_start, row_count, col_count, row_length):
    stream_key = mix_bits(mix_bits(drop_step[0] + jnp.int32(1013904223)) ^ drop_seed[0])
    row_ids = jnp.arange(row_count, dtype=jnp.int32) + row_start
    col_ids = jnp.arange(col_count, dtype=jnp.int32) + col_start
    flat_index = row_ids[:, None] * jnp.int32(row_length) + col_ids[None, :]
    hashed = mix_bits(flat_index ^ stream_key)
    return hashed & jnp.int32(16777215) < jnp.int32(15099494)


def gelu_parts(hidden_pre):
    inner_arg = gelu_coef * (hidden_pre + 0.044715 * hidden_pre * hidden_pre * hidden_pre)
    tanh_val = jnp.tanh(inner_arg)
    act_full = 0.5 * hidden_pre * (1.0 + tanh_val)
    gelu_slope = 0.5 * (1.0 + tanh_val) + 0.5 * hidden_pre * (
        1.0 - tanh_val * tanh_val
    ) * gelu_coef * (1.0 + 3.0 * 0.044715 * hidden_pre * hidden_pre)
    return (act_full, gelu_slope)


def dot(left, right, left_dim, right_dim):
    return lax.dot_general(
        left, right, (((left_dim,), (right_dim,)), ((), ())), preferred_element_type=F32
    )


def after(value, *others):
    return lax.optimization_barrier((value, *others))[0]


def partial_kernel(right_dim, half_ref, left_ref, w_ref, sum_ref, low_ref):
    part = dot(left_ref[...], w_ref[...], 1, right_dim)
    sum_ref[...] = part
    low_ref[...] = part.astype(BF16)


def partial_sum(half, left, weight, right_dim, chunk, chunks, width):
    tokens, feats = left.shape
    place = lambda g, half: jnp.where(g == 0, half[0], 1 - half[0]) * chunks + chunk
    if right_dim == 0:
        w_spec = pl.BlockSpec((feats, width), lambda g, half: (0, place(g, half)))
    else:
        w_spec = pl.BlockSpec((width, feats), lambda g, half: (place(g, half), 0))
    out = pl.BlockSpec((tokens, width), lambda g, half: (0, g))
    shape = (tokens, 2 * width)
    return pl.pallas_call(
        functools.partial(partial_kernel, right_dim),
        grid_spec=pltpu.PrefetchScalarGridSpec(
            num_scalar_prefetch=1,
            grid=(2,),
            in_specs=[pl.BlockSpec((tokens, feats), lambda g, half: (0, 0)), w_spec],
            out_specs=[out] * 2,
        ),
        out_shape=[jax.ShapeDtypeStruct(shape, F32), jax.ShapeDtypeStruct(shape, BF16)],
        compiler_params=pltpu.CompilerParams(vmem_limit_bytes=VMEM_LIMIT),
        cost_estimate=pl.CostEstimate(
            flops=4 * tokens * feats * width, bytes_accessed=4 * feats * width, transcendentals=0
        ),
        name="partial_sum",
    )(half, left, weight)


def input_kernel(first, half_ref, *refs):
    if first:
        pg_ref, w_ref, low_ref, high_ref = refs
    else:
        pg_ref, w_ref, low_acc_ref, high_acc_ref, low_ref, high_ref = refs
    part = dot(pg_ref[...], w_ref[...], 1, 1)
    rows = low_ref.shape[0]

    @pl.when(pl.program_id(0) == 0)
    def _():
        low_ref[...] = part[:rows] if first else low_acc_ref[...] + part[:rows]
        high_ref[...] = part[rows:] if first else high_acc_ref[...] + part[rows:]

    @pl.when(pl.program_id(0) != 0)
    def _():
        low_ref[...] += part[:rows]
        high_ref[...] += part[rows:]


def input_part(half, pg, w_in, acc, chunk, chunks, width):
    tokens, feats = pg.shape[0], w_in.shape[0]
    place = lambda g, half: jnp.where(g == 0, half[0], 1 - half[0]) * chunks + chunk
    whole = pl.BlockSpec((tokens // 2, feats), lambda g, half: (0, 0))
    first = acc is None
    return pl.pallas_call(
        functools.partial(input_kernel, first),
        grid_spec=pltpu.PrefetchScalarGridSpec(
            num_scalar_prefetch=1,
            grid=(2,),
            in_specs=[
                pl.BlockSpec((tokens, width), lambda g, half: (0, g)),
                pl.BlockSpec((feats, width), lambda g, half: (0, place(g, half))),
            ]
            + ([] if first else [whole] * 2),
            out_specs=[whole] * 2,
        ),
        out_shape=[jax.ShapeDtypeStruct((tokens // 2, feats), F32)] * 2,
        compiler_params=pltpu.CompilerParams(vmem_limit_bytes=VMEM_LIMIT),
        cost_estimate=pl.CostEstimate(
            flops=4 * tokens * feats * width, bytes_accessed=4 * feats * width, transcendentals=0
        ),
        name="input_part",
    )(half, pg, w_in, *(() if first else acc))


def weight_kernel(half_ref, xt_ref, s_ref, act_ref, act_far_ref, pg_ref, pg_far_ref, *refs):
    in_ref, out_ref = refs[-2:]
    pg = jnp.concatenate([pg_ref[...], pg_far_ref[...]], axis=0)
    in_ref[...] = dot(xt_ref[...], pg, 1, 0)
    act = jnp.concatenate([act_ref[...], act_far_ref[...]], axis=0)
    out_ref[...] = dot(act, s_ref[...], 0, 0)


def weight_part(half, xt, s_half, act, far, pg, totals, chunk, chunks, width):
    feats, all_tokens = xt.shape
    tokens = all_tokens // 2
    place = lambda g, half: jnp.where(g == 0, half[0], 1 - half[0]) * chunks + chunk
    first = totals is None
    return pl.pallas_call(
        weight_kernel,
        grid_spec=pltpu.PrefetchScalarGridSpec(
            num_scalar_prefetch=1,
            grid=(2,),
            in_specs=[
                pl.BlockSpec((feats // 2, all_tokens), lambda g, half: (g, 0)),
                pl.BlockSpec((all_tokens, feats // 2), lambda g, half: (0, 0)),
                pl.BlockSpec((tokens, width), lambda g, half: (0, g)),
                pl.BlockSpec((tokens, width), lambda g, half: (0, 1 - g)),
                pl.BlockSpec((tokens, width), lambda g, half: (0, 0)),
                pl.BlockSpec((tokens, width), lambda g, half: (0, 2)),
            ]
            + ([] if first else [pl.BlockSpec(memory_space=pl.ANY)] * 2),
            out_specs=[
                pl.BlockSpec((feats // 2, width), lambda g, half: (g, chunk)),
                pl.BlockSpec((width, feats // 2), lambda g, half: (place(g, half), 0)),
            ],
        ),
        out_shape=[
            jax.ShapeDtypeStruct((feats, chunks * width), F32),
            jax.ShapeDtypeStruct((2 * chunks * width, feats // 2), F32),
        ],
        input_output_aliases={} if first else {7: 0, 8: 1},
        compiler_params=pltpu.CompilerParams(vmem_limit_bytes=VMEM_LIMIT),
        cost_estimate=pl.CostEstimate(
            flops=8 * tokens * feats * width, bytes_accessed=8 * feats * width, transcendentals=0
        ),
        name="weight_part",
    )(half, xt, s_half, act, far, pg, far, *(() if first else totals))


def doubling_gather(value, axis, size):
    bit = size // 2
    while bit:
        got = lax.ppermute(value, axis, [(i, i ^ bit) for i in range(size)])
        value = jnp.concatenate([value, got], axis=0)
        bit //= 2
    return value


def halving_sum(keep, send, axis, size):
    bit = 1
    while True:
        got = lax.ppermute(send, axis, [(i, i ^ bit) for i in range(size)])
        bit *= 2
        if bit == size:
            return keep + got.astype(F32)
        rows = keep.shape[0] // 2
        send = (keep[rows:] + got[rows:].astype(F32)).astype(BF16)
        keep = keep[:rows] + got[:rows].astype(F32)


def per_device(sizes, layer_input, w_in, w_out, out_grad, drop_seed, drop_step):
    rows, cols, depths = sizes
    row, col, depth = lax.axis_index("row"), lax.axis_index("col"), lax.axis_index("depth")
    own_tokens, feats = layer_input.shape
    hidden = w_in.shape[1]
    assert rows == 4 and depths == 2 and hidden % 256 == 0
    lanes = hidden // 256
    chunks = max(k for k in range(1, CHUNKS + 1) if lanes % k == 0)
    width = hidden // 2 // chunks
    half = depth.astype(jnp.int32).reshape(1)
    swap = [(0, 1), (1, 0)]
    is_end = (row == 0) | (row == 3)
    inward, outward, across = [(0, 1), (3, 2)], [(1, 0), (2, 3)], [(1, 2), (2, 1)]

    keep_flags = keep_mask(
        drop_seed, drop_step, (depth * cols + col) * own_tokens, row * feats, own_tokens, feats, D
    )
    own_scaled = jnp.where(
        keep_flags, out_grad.astype(F32) * keep_scale, jnp.zeros((), F32)
    ).astype(BF16)
    x = doubling_gather(layer_input, "col", cols)
    s = doubling_gather(own_scaled, "col", cols)
    lefts, weights = (x, s), (w_in, w_out)

    part, low = {}, {}
    total, total_low = {}, {}
    made, done = {}, {}
    slope = {}
    got1, got2 = {}, {}

    def compute(q, t, gate):
        if t < chunks:
            part[q, t], low[q, t] = partial_sum(
                half if gate is None else after(half, gate[:8, :128]), lefts[q], weights[q], q, t, chunks, width
            )

    def send(q, t):
        pairs, payload = [], None
        if t < chunks:
            pairs, payload = inward, low[q, t]
        if t >= 2:
            pairs = pairs + outward
            payload = made[q, t - 2] if payload is None else jnp.where(is_end, payload, made[q, t - 2])
        got1[q, t] = lax.ppermute(payload, "row", pairs)
        if 1 <= t <= chunks:
            got2[q, t] = lax.ppermute(total_low[q, t - 1], "row", across)

    def receive(q, t):
        if t < chunks:
            total[q, t] = part[q, t] + got1[q, t].astype(F32)
            total_low[q, t] = total[q, t].astype(BF16)
        if 1 <= t <= chunks:
            whole = total[q, t - 1] + got2[q, t].astype(F32)
            if q == 0:
                act_full, slope[t - 1] = gelu_parts(whole)
                made[q, t - 1] = act_full.astype(BF16)
            else:
                made[q, t - 1] = (whole * slope[t - 1]).astype(BF16)
        if t >= 2:
            done[q, t - 2] = jnp.where(is_end, got1[q, t], made[q, t - 2])

    acc, totals = None, None
    far = {}
    compute(0, 0, None)
    compute(1, 0, None)
    s_half = xt = None
    steps = 2 * (chunks + 2)
    for u in range(steps + 1):
        q, t = u % 2, u // 2
        if u < steps:
            send(q, t)
        if u >= 1:
            q, t = (u - 1) % 2, (u - 1) // 2
            compute(q, t + 1, got1[q, t - 1] if t >= 1 else None)
            receive(q, t)
            if u == 3:
                s_split = s.reshape(s.shape[0], 2, feats // 2)
                s_mine = lax.dynamic_index_in_dim(s_split, depth, 1, keepdims=False)
                s_theirs = lax.dynamic_index_in_dim(s_split, 1 - depth, 1, keepdims=False)
                s_half = jnp.concatenate([s_mine, lax.ppermute(s_theirs, "depth", swap)], axis=0)
                xt = jnp.concatenate([x, lax.ppermute(x, "depth", swap)], axis=0).T
            if q == 1 and t >= 2:
                c = t - 2
                act, pg = done[0, c], done[1, c]
                both = jnp.concatenate([act, pg[:, width:]], axis=1)
                far[c] = lax.ppermute(both, "depth", swap)
                acc = input_part(half, pg, w_in, acc, c, chunks, width)
                totals = weight_part(half, xt, s_half, act, far[c], pg, totals, c, chunks, width)
    input_grad = halving_sum(*acc, "col", cols)
    return (input_grad, totals[0], totals[1])


def solution(mesh):
    placed = (
        P(("depth", "col"), "row"),
        P("row", "col"),
        P("col", "row"),
        P(("depth", "col"), "row"),
        P(),
        P(),
    )
    sizes = tuple(mesh.shape[name] for name in ("row", "col", "depth"))
    return jax.shard_map(
        functools.partial(per_device, sizes),
        mesh=mesh,
        in_specs=placed,
        out_specs=(
            P(("depth", "col"), "row"),
            P("row", ("col", "depth")),
            P("col", ("row", "depth")),
        ),
        check_vma=False,
    )
```

```python
import functools
import math

import jax
import jax.numpy as jnp
from jax import lax
from jax.experimental import pallas as pl
from jax.experimental.pallas import tpu as pltpu
from jax.sharding import PartitionSpec as P

D = 6144
CHUNKS = 8
SCALE = 2.0
MAIN, TAIL, TAILS = 4, 2, 0
VMEM_LIMIT = 93 * 512 * 1024

keep_scale = 1.0 / 0.9
gelu_coef = math.sqrt(2.0 / math.pi)

F32, BF16 = jnp.float32, jnp.bfloat16


def mix_bits(word_bits):
    word_bits = word_bits ^ lax.shift_right_logical(word_bits, jnp.int32(16))
    word_bits = word_bits * jnp.int32(2146121005)
    word_bits = word_bits ^ lax.shift_right_logical(word_bits, jnp.int32(15))
    word_bits = word_bits * jnp.int32(-2073254261)
    word_bits = word_bits ^ lax.shift_right_logical(word_bits, jnp.int32(16))
    return word_bits


def keep_mask(drop_seed, drop_step, row_start, col_start, row_count, col_count, row_length):
    stream_key = mix_bits(mix_bits(drop_step[0] + jnp.int32(1013904223)) ^ drop_seed[0])
    row_ids = jnp.arange(row_count, dtype=jnp.int32) + row_start
    col_ids = jnp.arange(col_count, dtype=jnp.int32) + col_start
    flat_index = row_ids[:, None] * jnp.int32(row_length) + col_ids[None, :]
    hashed = mix_bits(flat_index ^ stream_key)
    return hashed & jnp.int32(16777215) < jnp.int32(15099494)


def gelu_parts(hidden_pre):
    inner_arg = gelu_coef * (hidden_pre + 0.044715 * hidden_pre * hidden_pre * hidden_pre)
    tanh_val = jnp.tanh(inner_arg)
    act_full = 0.5 * hidden_pre * (1.0 + tanh_val)
    gelu_slope = 0.5 * (1.0 + tanh_val) + 0.5 * hidden_pre * (
        1.0 - tanh_val * tanh_val
    ) * gelu_coef * (1.0 + 3.0 * 0.044715 * hidden_pre * hidden_pre)
    return (act_full, gelu_slope)


def dot(left, right, left_dim, right_dim):
    return lax.dot_general(
        left, right, (((left_dim,), (right_dim,)), ((), ())), preferred_element_type=F32
    )


ANY = pl.BlockSpec(memory_space=pl.ANY)
HBM = pl.BlockSpec(memory_space=pltpu.HBM)


def call(kernel, grid, in_specs, out_specs, out_shape, cost, name, place, args, gate, aliases=None, scratch=()):
    count = len(args)

    def body(place_ref, *refs):
        kernel(place_ref, *refs[:count], *refs[count + len(gate) :])

    return pl.pallas_call(
        body,
        grid_spec=pltpu.PrefetchScalarGridSpec(
            num_scalar_prefetch=1,
            grid=grid,
            in_specs=list(in_specs) + [ANY] * len(gate),
            out_specs=out_specs,
            scratch_shapes=scratch,
        ),
        out_shape=out_shape,
        input_output_aliases=aliases or {},
        compiler_params=pltpu.CompilerParams(vmem_limit_bytes=VMEM_LIMIT),
        cost_estimate=pl.CostEstimate(flops=int(SCALE * cost * 1e9), bytes_accessed=1, transcendentals=0),
        name=name,
    )(place, *args, *gate)


def half_offset(place, mine, hidden, start):
    half = hidden // 2
    return pl.multiple_of(jnp.where(mine, place[0], 1 - place[0]) * half + start, 128)


def partial_sums(place, x, s, w_in, w_out, gate, start, count, width):
    tokens, feats = x.shape
    hidden = w_in.shape[1]

    def kernel(place_ref, x_ref, s_ref, w_in_ref, w_out_ref, *refs):
        outs, (in_buf, out_buf, sems) = refs[: 2 * count], refs[2 * count :]
        step = pl.program_id(0)

        def copies(i):
            at = half_offset(place_ref, i % 2 == 0, hidden, start + i // 2 * width)
            return (
                pltpu.make_async_copy(w_in_ref.at[:, pl.ds(at, width)], in_buf.at[i], sems.at[2 * i]),
                pltpu.make_async_copy(w_out_ref.at[pl.ds(at, width), :], out_buf.at[i], sems.at[2 * i + 1]),
            )

        @pl.when(step == 0)
        def _():
            for i in range(2 * count):
                for copy in copies(i):
                    copy.start()

        for i in range(2 * count):

            @pl.when(step == i)
            def _():
                of_in, of_out = copies(i)
                sum_ref, low_ref = outs[i // 2 * 2], outs[i // 2 * 2 + 1]
                h, a = 1 - i % 2, i % 2
                of_in.wait()
                part = dot(x_ref[...], in_buf[i], 1, 0)
                sum_ref[h] = part
                low_ref[h] = part.astype(BF16)
                of_out.wait()
                part = dot(s_ref[...], out_buf[i], 1, 1)
                sum_ref[a] = part
                low_ref[a] = part.astype(BF16)

    whole = pl.BlockSpec((tokens, feats), lambda step, place: (0, 0))
    outs = []
    for i in range(count):
        index = lambda step, place, i=i: (jnp.clip(step - 2 * i, 0, 1), 0, 0)
        outs += [pl.BlockSpec((2, tokens, width), index)] * 2
    shape = (4, tokens, width)
    return call(
        kernel,
        (2 * count,),
        [whole, whole, HBM, HBM],
        outs,
        [jax.ShapeDtypeStruct(shape, F32), jax.ShapeDtypeStruct(shape, BF16)] * count,
        4.0 * count,
        "partial_sums",
        place,
        (x, s, w_in, w_out),
        gate,
        scratch=[
            pltpu.VMEM((2 * count, feats, width), BF16),
            pltpu.VMEM((2 * count, width, feats), BF16),
            pltpu.SemaphoreType.DMA((4 * count,)),
        ],
    )


def add_end(place, own, got, gate, passed):
    _, tokens, width = own.shape

    def kernel(place_ref, own_ref, got_ref, *refs):
        sum_ref, low_ref = refs[len(passed) : len(passed) + 2]
        total = own_ref[...] + got_ref[...].astype(F32)
        sum_ref[...] = total
        low_ref[...] = total.astype(BF16)

    block = pl.BlockSpec((2, tokens, width), lambda g, place: (g, 0, 0))
    return call(
        kernel,
        (2,),
        [block, block] + [ANY] * len(passed),
        [block, block] + [ANY] * len(passed),
        [jax.ShapeDtypeStruct(own.shape, F32), jax.ShapeDtypeStruct(own.shape, BF16)]
        + [jax.ShapeDtypeStruct(p.shape, p.dtype) for p in passed],
        0.75,
        "add_end",
        place,
        (own, got, *passed),
        gate,
        {3 + i: 2 + i for i in range(len(passed))},
    )


def activate(place, total, got, gate):
    _, tokens, width = total.shape

    def kernel(place_ref, total_ref, got_ref, made_ref):
        g = pl.program_id(0)
        act_full, gelu_slope = gelu_parts(total_ref[1 - g] + got_ref[1 - g].astype(F32))
        made_ref[1 - g] = act_full.astype(BF16)
        made_ref[g] = ((total_ref[g] + got_ref[g].astype(F32)) * gelu_slope).astype(BF16)

    block = pl.BlockSpec((2, tokens, width), lambda g, place: (g, 0, 0))
    return call(
        kernel,
        (2,),
        [block, block],
        block,
        jax.ShapeDtypeStruct(total.shape, BF16),
        1.1,
        "activate",
        place,
        (total, got),
        gate,
    )


def choose(place, made, got, gate):
    count = len(made)
    _, tokens, width = made[0].shape

    def kernel(place_ref, *refs):
        for i in range(count):

            @pl.when(place_ref[1] == 0)
            def _():
                refs[-2][i] = refs[i][0]
                refs[-1][3 * i : 3 * i + 3] = refs[i][1:]

            @pl.when(place_ref[1] != 0)
            def _():
                refs[-2][i] = refs[count + i][0]
                refs[-1][3 * i : 3 * i + 3] = refs[count + i][1:]

    whole = pl.BlockSpec((4, tokens, width), lambda g, place: (0, 0, 0))
    shapes = [(count, tokens, width), (3 * count, tokens, width)]
    return call(
        kernel,
        (1,),
        [whole] * (2 * count),
        [pl.BlockSpec(shape, lambda g, place: (0, 0, 0)) for shape in shapes],
        [jax.ShapeDtypeStruct(shape, BF16) for shape in shapes],
        0.6,
        "choose",
        place,
        (*made, *got),
        gate,
    )


def gradients(place, first, three, far, w_in, xt, s_half, acc, totals, gate, start, count, width):
    tokens = first.shape[1]
    feats, hidden = w_in.shape
    rows = tokens // 2
    with_input, with_weights = acc is not None, far is not None
    fresh_input, fresh_weights = with_input and not acc, with_weights and not totals

    def kernel(place_ref, first_ref, three_ref, *refs):
        refs = list(refs)
        step = pl.program_id(0)
        g = step % 2
        if with_weights:
            far_ref, xt_ref, s_ref = refs[:3]
            del refs[:3]
        if with_input:
            w_ref, sems, buf = refs.pop(0), refs.pop(), refs.pop()
            if not fresh_input:
                acc_refs = refs[:2]
                del refs[:2]

            def copy(i):
                at = half_offset(place_ref, i % 2 == 0, hidden, start + i // 2 * width)
                return pltpu.make_async_copy(w_ref.at[:, pl.ds(at, width)], buf.at[i], sems.at[i])

            @pl.when(step == 0)
            def _():
                for i in range(2 * count):
                    copy(i).start()

        if with_weights and not fresh_weights:
            del refs[:2]
        if with_weights:
            in_ref, out_ref = refs[-2:]
            pg = jnp.concatenate([first_ref[0], far_ref[2]], axis=0)
            in_ref[...] = dot(xt_ref[...], pg, 1, 0)
            act = jnp.concatenate([three_ref[g], far_ref[1 - g]], axis=0)
            out_ref[...] = dot(act, s_ref[...], 0, 0)
        if with_input:
            for i in range(2 * count):

                @pl.when(step == i)
                def _():
                    copy(i).wait()
                    part = dot(three_ref[2] if i % 2 else first_ref[0], buf[i], 1, 1)
                    for k in range(2):
                        mine = part[k * rows : (k + 1) * rows]
                        if i == 0:
                            refs[k][...] = mine if fresh_input else acc_refs[k][...] + mine
                        else:
                            refs[k][...] += mine

    blocks = lambda n: pl.BlockSpec((n, tokens, width), lambda step, place: (step // 2, 0, 0))
    whole = pl.BlockSpec((rows, feats), lambda step, place: (0, 0))
    args, in_specs = [first, three], [blocks(1), blocks(3)]
    out_specs, out_shape, aliases, scratch = [], [], {}, []
    if with_weights:
        args += [far, xt, s_half]
        in_specs += [
            blocks(3),
            pl.BlockSpec((feats // 2, 2 * tokens), lambda step, place: (step % 2, 0)),
            pl.BlockSpec((2 * tokens, feats // 2), lambda step, place: (0, 0)),
        ]
    if with_input:
        args += [w_in, *acc]
        in_specs += [HBM] + [whole] * len(acc)
        out_specs += [whole] * 2
        out_shape += [jax.ShapeDtypeStruct((rows, feats), F32)] * 2
        scratch = [
            pltpu.VMEM((2 * count, feats, width), BF16),
            pltpu.SemaphoreType.DMA((2 * count,)),
        ]
    if with_weights:
        per_half, first_chunk = hidden // 2 // width, start // width

        def out_place(step, place):
            half = jnp.where(step % 2 == 0, place[0], 1 - place[0])
            return half * per_half + first_chunk + step // 2, 0

        for total in totals:
            aliases[1 + len(args)] = len(out_shape) + len(aliases)
            args += [total]
            in_specs += [HBM]
        out_specs += [
            pl.BlockSpec((feats // 2, width), lambda step, place: (step % 2, first_chunk + step // 2)),
            pl.BlockSpec((width, feats // 2), out_place),
        ]
        out_shape += [pltpu.HBM((feats, hidden // 2), F32), pltpu.HBM((hidden, feats // 2), F32)]
    outs = call(
        kernel,
        (2 * count,),
        in_specs,
        out_specs,
        out_shape,
        2.9 * (with_input + with_weights),
        "gradients",
        place,
        args,
        gate,
        aliases,
        scratch,
    )
    return (tuple(outs[:2]) if with_input else None), (tuple(outs[-2:]) if with_weights else totals)


def plan(units):
    tail = TAIL * TAILS
    main = units - tail
    if main > 0 and main % MAIN == 0 and main % TAIL == 0 and units % MAIN == 0 and units % TAIL == 0:
        widths = [MAIN] * (main // MAIN) + [TAIL] * TAILS
    else:
        count = max(k for k in range(1, CHUNKS + 1) if units % k == 0)
        widths = [units // count] * count
    return [(128 * sum(widths[:i]), 128 * width) for i, width in enumerate(widths)]


def doubling_gather(value, axis, size):
    bit = size // 2
    while bit:
        got = lax.ppermute(value, axis, [(i, i ^ bit) for i in range(size)])
        value = jnp.concatenate([value, got], axis=0)
        bit //= 2
    return value


def halving_sum(keep, send, axis, size):
    bit = 1
    while True:
        got = lax.ppermute(send, axis, [(i, i ^ bit) for i in range(size)])
        bit *= 2
        if bit == size:
            return keep + got.astype(F32)
        rows = keep.shape[0] // 2
        send = (keep[rows:] + got[rows:].astype(F32)).astype(BF16)
        keep = keep[:rows] + got[:rows].astype(F32)


def per_device(sizes, layer_input, w_in, w_out, out_grad, drop_seed, drop_step):
    rows, cols, depths = sizes
    row, col, depth = lax.axis_index("row"), lax.axis_index("col"), lax.axis_index("depth")
    own_tokens, feats = layer_input.shape
    hidden = w_in.shape[1]
    assert rows == 4 and depths == 2 and hidden % 256 == 0
    chunks = plan(hidden // 256)
    swap = [(0, 1), (1, 0)]
    is_end = (row == 0) | (row == 3)
    place = jnp.stack([depth, is_end]).astype(jnp.int32)
    inward, outward, across = [(0, 1), (3, 2)], [(1, 0), (2, 3)], [(1, 2), (2, 1)]

    keep_flags = keep_mask(
        drop_seed, drop_step, (depth * cols + col) * own_tokens, row * feats, own_tokens, feats, D
    )
    own_scaled = jnp.where(
        keep_flags, out_grad.astype(F32) * keep_scale, jnp.zeros((), F32)
    ).astype(BF16)
    x = doubling_gather(layer_input, "col", cols)
    s = doubling_gather(own_scaled, "col", cols)

    s_split = s.reshape(s.shape[0], 2, feats // 2)
    s_mine = lax.dynamic_index_in_dim(s_split, depth, 1, keepdims=False)
    s_theirs = lax.dynamic_index_in_dim(s_split, 1 - depth, 1, keepdims=False)
    s_half = jnp.concatenate([s_mine, lax.ppermute(s_theirs, "depth", swap)], axis=0)
    xt = jnp.concatenate([x, lax.ppermute(x, "depth", swap)], axis=0).T

    own, low, total, made, got, first, three, far = ({} for _ in range(8))
    acc, totals = (), ()
    last = ()
    n = len(chunks)
    to_prepare, c = [(0, 1)], 1
    while c < n:
        count = 2 if c + 1 < n and chunks[c][1] == chunks[c + 1][1] else 1
        to_prepare.append((c, count))
        c += count

    def prepare():
        nonlocal last
        if to_prepare:
            start, count = to_prepare.pop(0)
            sums = partial_sums(place, x, s, w_in, w_out, last, chunks[start][0], count, chunks[start][1])
            for i in range(count):
                own[start + i], low[start + i] = sums[2 * i], sums[2 * i + 1]
            last = (sums[-1],)

    def finish(c, acc, totals, part=None):
        return gradients(
            place, first[c], three[c], None if part == "input" else far[c], w_in, xt, s_half,
            None if part == "weights" else acc, totals, last, chunks[c][0], 1, chunks[c][1],
        )

    prepare()
    prepare()
    prepare()
    todo = []
    for c in range(n + 2):
        if c < n:
            got_end = lax.ppermute(low[c], "row", inward)
            while to_prepare and c + 2 < n and c + 2 not in low:
                prepare()
            passed = (low[c + 2],) if c + 2 < n else ()
            total[c], low[c], *passed = add_end(place, own[c], got_end, last, passed)
            if passed:
                (low[c + 2],) = passed
            last = (low[c],)
        if 1 <= c <= n:
            got_across = lax.ppermute(low[c - 1], "row", across)
            made[c - 1] = activate(place, total[c - 1], got_across, last)
            last = (made[c - 1],)
        if c >= 2:
            got[c - 2] = lax.ppermute(made[c - 2], "row", outward)
            first[c - 2], three[c - 2] = choose(place, [made[c - 2]], [got[c - 2]], last)
            far[c - 2] = lax.ppermute(three[c - 2], "depth", swap)
            todo.append(c - 2)
            last = (first[c - 2],)
        prepare()
        if c == 1:
            last += (xt, s_half)
        if len(todo) > 1 and c < n + 1:
            acc, totals = finish(todo.pop(0), acc, totals)
            last = (totals[0],)
        if c == n:
            acc, _ = finish(todo[0], acc, (), "input")
            last = (acc[1],)
        if c == n + 1:
            acc, _ = finish(todo[1], acc, (), "input")
            last = (acc[1],)
    for c in todo:
        _, totals = finish(c, None, totals, "weights")
        last = ()
    input_grad = halving_sum(*acc, "col", cols)
    return (input_grad, totals[0], totals[1])


def solution(mesh):
    placed = (
        P(("depth", "col"), "row"),
        P("row", "col"),
        P("col", "row"),
        P(("depth", "col"), "row"),
        P(),
        P(),
    )
    sizes = tuple(mesh.shape[name] for name in ("row", "col", "depth"))
    return jax.shard_map(
        functools.partial(per_device, sizes),
        mesh=mesh,
        in_specs=placed,
        out_specs=(
            P(("depth", "col"), "row"),
            P("row", ("col", "depth")),
            P("col", ("row", "depth")),
        ),
        check_vma=False,
    )
```

```python
import functools
import math

import jax
import jax.numpy as jnp
from jax import lax
from jax.experimental import pallas as pl
from jax.experimental.pallas import tpu as pltpu
from jax.sharding import PartitionSpec as P

D = 6144
CHUNKS = 8
SCALE = 1.0
MAIN, TAIL, TAILS = 4, 2, 0
VMEM_LIMIT = 28 * 1024 * 1024

keep_scale = 1.0 / 0.9
gelu_coef = math.sqrt(2.0 / math.pi)

F32, BF16 = jnp.float32, jnp.bfloat16


def mix_bits(word_bits):
    word_bits = word_bits ^ lax.shift_right_logical(word_bits, jnp.int32(16))
    word_bits = word_bits * jnp.int32(2146121005)
    word_bits = word_bits ^ lax.shift_right_logical(word_bits, jnp.int32(15))
    word_bits = word_bits * jnp.int32(-2073254261)
    word_bits = word_bits ^ lax.shift_right_logical(word_bits, jnp.int32(16))
    return word_bits


def keep_mask(drop_seed, drop_step, row_start, col_start, row_count, col_count, row_length):
    stream_key = mix_bits(mix_bits(drop_step[0] + jnp.int32(1013904223)) ^ drop_seed[0])
    row_ids = jnp.arange(row_count, dtype=jnp.int32) + row_start
    col_ids = jnp.arange(col_count, dtype=jnp.int32) + col_start
    flat_index = row_ids[:, None] * jnp.int32(row_length) + col_ids[None, :]
    hashed = mix_bits(flat_index ^ stream_key)
    return hashed & jnp.int32(16777215) < jnp.int32(15099494)


def gelu_parts(hidden_pre):
    inner_arg = gelu_coef * (hidden_pre + 0.044715 * hidden_pre * hidden_pre * hidden_pre)
    tanh_val = jnp.tanh(inner_arg)
    act_full = 0.5 * hidden_pre * (1.0 + tanh_val)
    gelu_slope = 0.5 * (1.0 + tanh_val) + 0.5 * hidden_pre * (
        1.0 - tanh_val * tanh_val
    ) * gelu_coef * (1.0 + 3.0 * 0.044715 * hidden_pre * hidden_pre)
    return (act_full, gelu_slope)


def dot(left, right, left_dim, right_dim):
    return lax.dot_general(
        left, right, (((left_dim,), (right_dim,)), ((), ())), preferred_element_type=F32
    )


ANY = pl.BlockSpec(memory_space=pl.ANY)
HBM = pl.BlockSpec(memory_space=pltpu.HBM)


def call(kernel, grid, in_specs, out_specs, out_shape, cost, name, place, args, gate, aliases=None, scratch=()):
    count = len(args)

    def body(place_ref, *refs):
        kernel(place_ref, *refs[:count], *refs[count + len(gate) :])

    return pl.pallas_call(
        body,
        grid_spec=pltpu.PrefetchScalarGridSpec(
            num_scalar_prefetch=1,
            grid=grid,
            in_specs=list(in_specs) + [ANY] * len(gate),
            out_specs=out_specs,
            scratch_shapes=scratch,
        ),
        out_shape=out_shape,
        input_output_aliases=aliases or {},
        compiler_params=pltpu.CompilerParams(vmem_limit_bytes=VMEM_LIMIT),
        cost_estimate=pl.CostEstimate(flops=int(SCALE * cost * 1e9), bytes_accessed=1, transcendentals=0),
        name=name,
    )(place, *args, *gate)


def in_hbm(value):
    return pltpu.with_memory_space_constraint(value, pltpu.HBM)


def half_offset(place, mine, hidden, start):
    half = hidden // 2
    return pl.multiple_of(jnp.where(mine, place[0], 1 - place[0]) * half + start, 128)


def partial_sums(place, both, w_in, w_out, gate, start, count, width):
    _, tokens, feats = both.shape
    hidden = w_in.shape[1]

    def kernel(place_ref, x_ref, s_ref, w_in_ref, w_out_ref, *refs):
        outs, (in_buf, out_buf, sems) = refs[: 2 * count], refs[2 * count :]
        step = pl.program_id(0)

        def copies(i):
            at = half_offset(place_ref, i % 2 == 0, hidden, start + i // 2 * width)
            return (
                pltpu.make_async_copy(w_in_ref.at[:, pl.ds(at, width)], in_buf.at[i], sems.at[2 * i]),
                pltpu.make_async_copy(w_out_ref.at[pl.ds(at, width), :], out_buf.at[i], sems.at[2 * i + 1]),
            )

        @pl.when(step == 0)
        def _():
            for i in range(2 * count):
                for copy in copies(i):
                    copy.start()

        for i in range(2 * count):

            @pl.when(step == i)
            def _():
                of_in, of_out = copies(i)
                sum_ref, low_ref = outs[i // 2 * 2], outs[i // 2 * 2 + 1]
                h, a = 1 - i % 2, i % 2
                of_in.wait()
                part = dot(x_ref[0], in_buf[i], 1, 0)
                sum_ref[h] = part
                low_ref[h] = part.astype(BF16)
                of_out.wait()
                part = dot(s_ref[0], out_buf[i], 1, 1)
                sum_ref[a] = part
                low_ref[a] = part.astype(BF16)

    part_of = lambda k: pl.BlockSpec((1, tokens, feats), lambda step, place: (k, 0, 0))
    outs = []
    for i in range(count):
        index = lambda step, place, i=i: (jnp.clip(step - 2 * i, 0, 1), 0, 0)
        outs += [pl.BlockSpec((2, tokens, width), index)] * 2
    shape = (4, tokens, width)
    return call(
        kernel,
        (2 * count,),
        [part_of(0), part_of(1), HBM, HBM],
        outs,
        [jax.ShapeDtypeStruct(shape, F32), jax.ShapeDtypeStruct(shape, BF16)] * count,
        4.0 * count,
        "partial_sums",
        place,
        (both, both, w_in, w_out),
        gate,
        scratch=[
            pltpu.VMEM((2 * count, feats, width), BF16),
            pltpu.VMEM((2 * count, width, feats), BF16),
            pltpu.SemaphoreType.DMA((4 * count,)),
        ],
    )


def all_tokens(place, both, far):
    _, tokens, feats = both.shape
    part = 256

    def kernel(place_ref, x_ref, x_far_ref, s_ref, s_far_ref, xt_ref, half_ref):
        xt_ref[...] = jnp.concatenate([x_ref[0], x_far_ref[0]], axis=0).T
        half_ref[:tokens] = s_ref[0]
        half_ref[tokens:] = s_far_ref[0]

    x_part = pl.BlockSpec((1, tokens, part), lambda step, place: (0, 0, step))
    s_part = pl.BlockSpec((1, tokens, feats // 2), lambda step, place: (1, 0, place[0]))
    return call(
        kernel,
        (feats // part,),
        [x_part, x_part, s_part, s_part],
        [
            pl.BlockSpec((part, 2 * tokens), lambda step, place: (step, 0)),
            pl.BlockSpec((2 * tokens, feats // 2), lambda step, place: (0, 0)),
        ],
        [
            jax.ShapeDtypeStruct((feats, 2 * tokens), BF16),
            jax.ShapeDtypeStruct((2 * tokens, feats // 2), BF16),
        ],
        2.0,
        "all_tokens",
        place,
        (both, far, both, far),
        (),
    )


def add_end(place, own, got, gate, passed):
    _, tokens, width = own.shape

    def kernel(place_ref, own_ref, got_ref, *refs):
        sum_ref, low_ref = refs[len(passed) : len(passed) + 2]
        total = own_ref[...] + got_ref[...].astype(F32)
        sum_ref[...] = total
        low_ref[...] = total.astype(BF16)

    block = pl.BlockSpec((2, tokens, width), lambda g, place: (g, 0, 0))
    return call(
        kernel,
        (2,),
        [block, block] + [ANY] * len(passed),
        [block, block] + [ANY] * len(passed),
        [jax.ShapeDtypeStruct(own.shape, F32), jax.ShapeDtypeStruct(own.shape, BF16)]
        + [jax.ShapeDtypeStruct(p.shape, p.dtype) for p in passed],
        0.75,
        "add_end",
        place,
        (own, got, *passed),
        gate,
        {3 + i: 2 + i for i in range(len(passed))},
    )


def activate(place, total, got, gate):
    _, tokens, width = total.shape

    def kernel(place_ref, total_ref, got_ref, made_ref):
        g = pl.program_id(0)
        act_full, gelu_slope = gelu_parts(total_ref[1 - g] + got_ref[1 - g].astype(F32))
        made_ref[1 - g] = act_full.astype(BF16)
        made_ref[g] = ((total_ref[g] + got_ref[g].astype(F32)) * gelu_slope).astype(BF16)

    block = pl.BlockSpec((2, tokens, width), lambda g, place: (g, 0, 0))
    return call(
        kernel,
        (2,),
        [block, block],
        block,
        jax.ShapeDtypeStruct(total.shape, BF16),
        1.1,
        "activate",
        place,
        (total, got),
        gate,
    )


def choose(place, made, got, gate):
    count = len(made)
    _, tokens, width = made[0].shape

    def kernel(place_ref, *refs):
        for i in range(count):

            @pl.when(place_ref[1] == 0)
            def _():
                refs[-2][i] = refs[i][0]
                refs[-1][3 * i : 3 * i + 3] = refs[i][1:]

            @pl.when(place_ref[1] != 0)
            def _():
                refs[-2][i] = refs[count + i][0]
                refs[-1][3 * i : 3 * i + 3] = refs[count + i][1:]

    whole = pl.BlockSpec((4, tokens, width), lambda g, place: (0, 0, 0))
    shapes = [(count, tokens, width), (3 * count, tokens, width)]
    return call(
        kernel,
        (1,),
        [whole] * (2 * count),
        [pl.BlockSpec(shape, lambda g, place: (0, 0, 0)) for shape in shapes],
        [jax.ShapeDtypeStruct(shape, BF16) for shape in shapes],
        0.6,
        "choose",
        place,
        (*made, *got),
        gate,
    )


def gradients(place, first, three, far, w_in, xt, s_half, acc, totals, gate, start, count, width):
    tokens = first.shape[1]
    feats, hidden = w_in.shape
    rows = tokens // 2
    with_input, with_weights = acc is not None, far is not None
    fresh_input, fresh_weights = with_input and not acc, with_weights and not totals

    def kernel(place_ref, first_ref, three_ref, *refs):
        refs = list(refs)
        step = pl.program_id(0)
        g = step % 2
        if with_weights:
            far_ref, xt_ref, s_ref = refs[:3]
            del refs[:3]
        if with_input:
            w_ref, sems, buf = refs.pop(0), refs.pop(), refs.pop()
            if not fresh_input:
                acc_refs = refs[:2]
                del refs[:2]

            def copy(i):
                at = half_offset(place_ref, i % 2 == 0, hidden, start + i // 2 * width)
                return pltpu.make_async_copy(w_ref.at[:, pl.ds(at, width)], buf.at[i], sems.at[i])

            @pl.when(step == 0)
            def _():
                for i in range(2 * count):
                    copy(i).start()

        if with_weights and not fresh_weights:
            del refs[:2]
        if with_weights:
            in_ref, out_ref = refs[-2:]
            pg = jnp.concatenate([first_ref[0], far_ref[2]], axis=0)
            in_ref[...] = dot(xt_ref[...], pg, 1, 0)
            act = jnp.concatenate([three_ref[g], far_ref[1 - g]], axis=0)
            out_ref[...] = dot(act, s_ref[...], 0, 0)
        if with_input:
            for i in range(2 * count):

                @pl.when(step == i)
                def _():
                    copy(i).wait()
                    part = dot(three_ref[2] if i % 2 else first_ref[0], buf[i], 1, 1)
                    for k in range(2):
                        mine = part[k * rows : (k + 1) * rows]
                        if i == 0:
                            refs[k][...] = mine if fresh_input else acc_refs[k][...] + mine
                        else:
                            refs[k][...] += mine

    blocks = lambda n: pl.BlockSpec((n, tokens, width), lambda step, place: (step // 2, 0, 0))
    whole = pl.BlockSpec((rows, feats), lambda step, place: (0, 0))
    args, in_specs = [first, three], [blocks(1), blocks(3)]
    out_specs, out_shape, aliases, scratch = [], [], {}, []
    if with_weights:
        args += [far, xt, s_half]
        in_specs += [
            blocks(3),
            pl.BlockSpec((feats // 2, 2 * tokens), lambda step, place: (step % 2, 0)),
            pl.BlockSpec((2 * tokens, feats // 2), lambda step, place: (0, 0)),
        ]
    if with_input:
        args += [w_in, *acc]
        in_specs += [HBM] + [whole] * len(acc)
        out_specs += [whole] * 2
        out_shape += [jax.ShapeDtypeStruct((rows, feats), F32)] * 2
        scratch = [
            pltpu.VMEM((2 * count, feats, width), BF16),
            pltpu.SemaphoreType.DMA((2 * count,)),
        ]
    if with_weights:
        per_half, first_chunk = hidden // 2 // width, start // width

        def out_place(step, place):
            half = jnp.where(step % 2 == 0, place[0], 1 - place[0])
            return half * per_half + first_chunk + step // 2, 0

        for total in totals:
            aliases[1 + len(args)] = len(out_shape) + len(aliases)
            args += [in_hbm(total)]
            in_specs += [HBM]
        out_specs += [
            pl.BlockSpec((feats // 2, width), lambda step, place: (step % 2, first_chunk + step // 2)),
            pl.BlockSpec((width, feats // 2), out_place),
        ]
        out_shape += [pltpu.HBM((feats, hidden // 2), F32), pltpu.HBM((hidden, feats // 2), F32)]
    outs = call(
        kernel,
        (2 * count,),
        in_specs,
        out_specs,
        out_shape,
        5.8 if with_input and with_weights else 20.0,
        "gradients",
        place,
        args,
        gate,
        aliases,
        scratch,
    )
    return (tuple(outs[:2]) if with_input else None), (tuple(outs[-2:]) if with_weights else totals)


def plan(units):
    tail = TAIL * TAILS
    main = units - tail
    if main > 0 and main % MAIN == 0 and main % TAIL == 0 and units % MAIN == 0 and units % TAIL == 0:
        widths = [MAIN] * (main // MAIN) + [TAIL] * TAILS
    else:
        count = max(k for k in range(1, CHUNKS + 1) if units % k == 0)
        widths = [units // count] * count
    return [(128 * sum(widths[:i]), 128 * width) for i, width in enumerate(widths)]


def doubling_gather(value, axis, size):
    bit = size // 2
    while bit:
        got = lax.ppermute(value, axis, [(i, i ^ bit) for i in range(size)])
        value = jnp.concatenate([value, got], axis=1)
        bit //= 2
    return value


def halving_sum(keep, send, axis, size):
    bit = 1
    while True:
        got = lax.ppermute(send, axis, [(i, i ^ bit) for i in range(size)])
        bit *= 2
        if bit == size:
            return keep + got.astype(F32)
        rows = keep.shape[0] // 2
        send = (keep[rows:] + got[rows:].astype(F32)).astype(BF16)
        keep = keep[:rows] + got[:rows].astype(F32)


def per_device(sizes, layer_input, w_in, w_out, out_grad, drop_seed, drop_step):
    rows, cols, depths = sizes
    row, col, depth = lax.axis_index("row"), lax.axis_index("col"), lax.axis_index("depth")
    own_tokens, feats = layer_input.shape
    hidden = w_in.shape[1]
    assert rows == 4 and depths == 2 and hidden % 256 == 0
    chunks = plan(hidden // 256)
    w_in, w_out = in_hbm(w_in), in_hbm(w_out)
    swap = [(0, 1), (1, 0)]
    is_end = (row == 0) | (row == 3)
    place = jnp.stack([depth, is_end]).astype(jnp.int32)
    inward, outward, across = [(0, 1), (3, 2)], [(1, 0), (2, 3)], [(1, 2), (2, 1)]

    keep_flags = keep_mask(
        drop_seed, drop_step, (depth * cols + col) * own_tokens, row * feats, own_tokens, feats, D
    )
    own_scaled = jnp.where(
        keep_flags, out_grad.astype(F32) * keep_scale, jnp.zeros((), F32)
    ).astype(BF16)
    both = doubling_gather(jnp.stack([layer_input, own_scaled]), "col", cols)
    xt, s_half = all_tokens(place, both, lax.ppermute(both, "depth", swap))

    own, low, total, made, got, first, three, far = ({} for _ in range(8))
    acc, totals = (), ()
    last = ()
    n = len(chunks)
    to_prepare, c = [], 0
    while c < n:
        count = 2 if c >= 2 and c + 1 < n and chunks[c][1] == chunks[c + 1][1] else 1
        to_prepare.append((c, count))
        c += count
    to_prepare[1:3] = to_prepare[2:0:-1]

    def prepare():
        nonlocal last
        if to_prepare:
            start, count = to_prepare.pop(0)
            sums = partial_sums(place, both, w_in, w_out, last, chunks[start][0], count, chunks[start][1])
            for i in range(count):
                own[start + i], low[start + i] = sums[2 * i], sums[2 * i + 1]
            last = (sums[-1],)

    def finish(c, acc, totals, part=None):
        return gradients(
            place, first[c], three[c], None if part == "input" else far[c], w_in, xt, s_half,
            None if part == "weights" else acc, totals, last, chunks[c][0], 1, chunks[c][1],
        )

    prepare()
    prepare()
    prepare()
    todo = []
    for c in range(n + 2):
        if c < n:
            got_end = lax.ppermute(low[c], "row", inward)
            while to_prepare and c + 2 < n and c + 2 not in low:
                prepare()
            passed = (low[c + 2],) if c + 2 < n else ()
            total[c], low[c], *passed = add_end(place, own[c], got_end, last, passed)
            if passed:
                (low[c + 2],) = passed
            last = (low[c],)
        if 1 <= c <= n:
            got_across = lax.ppermute(low[c - 1], "row", across)
            made[c - 1] = activate(place, total[c - 1], got_across, last)
            last = (made[c - 1],)
        if c >= 2:
            got[c - 2] = lax.ppermute(made[c - 2], "row", outward)
            first[c - 2], three[c - 2] = choose(place, [made[c - 2]], [got[c - 2]], last)
            far[c - 2] = lax.ppermute(three[c - 2], "depth", swap)
            todo.append(c - 2)
            last = (first[c - 2],)
        prepare()
        if c == 1:
            last += (xt, s_half)
        if len(todo) > 1 and c < n + 1:
            acc, totals = finish(todo.pop(0), acc, totals)
            last = (acc[1],)
        if c == n:
            acc, _ = finish(todo[0], acc, (), "input")
            last = (acc[1],)
        if c == n + 1:
            acc, _ = finish(todo[1], acc, (), "input")
            last = (acc[1],)
    for c in todo:
        _, totals = finish(c, None, totals, "weights")
        last = ()
    input_grad = halving_sum(*acc, "col", cols)
    return (input_grad, totals[0], totals[1])


def solution(mesh):
    placed = (
        P(("depth", "col"), "row"),
        P("row", "col"),
        P("col", "row"),
        P(("depth", "col"), "row"),
        P(),
        P(),
    )
    sizes = tuple(mesh.shape[name] for name in ("row", "col", "depth"))
    return jax.shard_map(
        functools.partial(per_device, sizes),
        mesh=mesh,
        in_specs=placed,
        out_specs=(
            P(("depth", "col"), "row"),
            P("row", ("col", "depth")),
            P("col", ("row", "depth")),
        ),
        check_vma=False,
    )
```

```python
import functools
import math

import jax
import jax.numpy as jnp
from jax import lax
from jax.experimental import pallas as pl
from jax.experimental.pallas import tpu as pltpu
from jax.sharding import PartitionSpec as P

D = 6144
CHUNKS = 8
SCALE = 1.0
MAIN, TAIL, TAILS = 4, 2, 0
VMEM_LIMIT = 28 * 1024 * 1024

keep_scale = 1.0 / 0.9
gelu_coef = math.sqrt(2.0 / math.pi)

F32, BF16 = jnp.float32, jnp.bfloat16


def mix_bits(word_bits):
    word_bits = word_bits ^ lax.shift_right_logical(word_bits, jnp.int32(16))
    word_bits = word_bits * jnp.int32(2146121005)
    word_bits = word_bits ^ lax.shift_right_logical(word_bits, jnp.int32(15))
    word_bits = word_bits * jnp.int32(-2073254261)
    word_bits = word_bits ^ lax.shift_right_logical(word_bits, jnp.int32(16))
    return word_bits


def keep_mask(drop_seed, drop_step, row_start, col_start, row_count, col_count, row_length):
    stream_key = mix_bits(mix_bits(drop_step[0] + jnp.int32(1013904223)) ^ drop_seed[0])
    row_ids = jnp.arange(row_count, dtype=jnp.int32) + row_start
    col_ids = jnp.arange(col_count, dtype=jnp.int32) + col_start
    flat_index = row_ids[:, None] * jnp.int32(row_length) + col_ids[None, :]
    hashed = mix_bits(flat_index ^ stream_key)
    return hashed & jnp.int32(16777215) < jnp.int32(15099494)


def gelu_parts(hidden_pre):
    inner_arg = gelu_coef * (hidden_pre + 0.044715 * hidden_pre * hidden_pre * hidden_pre)
    tanh_val = jnp.tanh(inner_arg)
    act_full = 0.5 * hidden_pre * (1.0 + tanh_val)
    gelu_slope = 0.5 * (1.0 + tanh_val) + 0.5 * hidden_pre * (
        1.0 - tanh_val * tanh_val
    ) * gelu_coef * (1.0 + 3.0 * 0.044715 * hidden_pre * hidden_pre)
    return (act_full, gelu_slope)


def dot(left, right, left_dim, right_dim):
    return lax.dot_general(
        left, right, (((left_dim,), (right_dim,)), ((), ())), preferred_element_type=F32
    )


ANY = pl.BlockSpec(memory_space=pl.ANY)
HBM = pl.BlockSpec(memory_space=pltpu.HBM)


def call(kernel, grid, in_specs, out_specs, out_shape, cost, name, place, args, gate, aliases=None, scratch=()):
    count = len(args)

    def body(place_ref, *refs):
        kernel(place_ref, *refs[:count], *refs[count + len(gate) :])

    return pl.pallas_call(
        body,
        grid_spec=pltpu.PrefetchScalarGridSpec(
            num_scalar_prefetch=1,
            grid=grid,
            in_specs=list(in_specs) + [ANY] * len(gate),
            out_specs=out_specs,
            scratch_shapes=scratch,
        ),
        out_shape=out_shape,
        input_output_aliases=aliases or {},
        compiler_params=pltpu.CompilerParams(vmem_limit_bytes=VMEM_LIMIT),
        cost_estimate=pl.CostEstimate(flops=int(SCALE * cost * 1e9), bytes_accessed=1, transcendentals=0),
        name=name,
    )(place, *args, *gate)


def in_hbm(value):
    return pltpu.with_memory_space_constraint(value, pltpu.HBM)


def half_offset(place, mine, hidden, start):
    half = hidden // 2
    return pl.multiple_of(jnp.where(mine, place[0], 1 - place[0]) * half + start, 128)


def partial_sums(place, both, w_in, w_out, gate, start, count, width):
    _, tokens, feats = both.shape
    hidden = w_in.shape[1]

    def kernel(place_ref, x_ref, s_ref, w_in_ref, w_out_ref, *refs):
        outs, (in_buf, out_buf, sems) = refs[: 2 * count], refs[2 * count :]
        step = pl.program_id(0)

        def copies(i):
            at = half_offset(place_ref, i % 2 == 0, hidden, start + i // 2 * width)
            return (
                pltpu.make_async_copy(w_in_ref.at[:, pl.ds(at, width)], in_buf.at[i], sems.at[2 * i]),
                pltpu.make_async_copy(w_out_ref.at[pl.ds(at, width), :], out_buf.at[i], sems.at[2 * i + 1]),
            )

        @pl.when(step == 0)
        def _():
            for i in range(2 * count):
                for copy in copies(i):
                    copy.start()

        for i in range(2 * count):

            @pl.when(step == i)
            def _():
                of_in, of_out = copies(i)
                sum_ref, low_ref = outs[i // 2 * 2], outs[i // 2 * 2 + 1]
                h, a = 1 - i % 2, i % 2
                of_in.wait()
                part = dot(x_ref[0], in_buf[i], 1, 0)
                sum_ref[h] = part
                low_ref[h] = part.astype(BF16)
                of_out.wait()
                part = dot(s_ref[0], out_buf[i], 1, 1)
                sum_ref[a] = part
                low_ref[a] = part.astype(BF16)

    part_of = lambda k: pl.BlockSpec((1, tokens, feats), lambda step, place: (k, 0, 0))
    outs = []
    for i in range(count):
        index = lambda step, place, i=i: (jnp.clip(step - 2 * i, 0, 1), 0, 0)
        outs += [pl.BlockSpec((2, tokens, width), index)] * 2
    shape = (4, tokens, width)
    return call(
        kernel,
        (2 * count,),
        [part_of(0), part_of(1), HBM, HBM],
        outs,
        [jax.ShapeDtypeStruct(shape, F32), jax.ShapeDtypeStruct(shape, BF16)] * count,
        4.0 * count,
        "partial_sums",
        place,
        (both, both, w_in, w_out),
        gate,
        scratch=[
            pltpu.VMEM((2 * count, feats, width), BF16),
            pltpu.VMEM((2 * count, width, feats), BF16),
            pltpu.SemaphoreType.DMA((4 * count,)),
        ],
    )


def all_tokens(place, both, far, gate):
    _, tokens, feats = both.shape
    part = 256

    def kernel(place_ref, x_ref, x_far_ref, s_ref, s_far_ref, xt_ref, half_ref):
        xt_ref[...] = jnp.concatenate([x_ref[0], x_far_ref[0]], axis=0).T
        half_ref[:tokens] = s_ref[0]
        half_ref[tokens:] = s_far_ref[0]

    x_part = pl.BlockSpec((1, tokens, part), lambda step, place: (0, 0, step))
    s_part = pl.BlockSpec((1, tokens, feats // 2), lambda step, place: (1, 0, place[0]))
    return call(
        kernel,
        (feats // part,),
        [x_part, x_part, s_part, s_part],
        [
            pl.BlockSpec((part, 2 * tokens), lambda step, place: (step, 0)),
            pl.BlockSpec((2 * tokens, feats // 2), lambda step, place: (0, 0)),
        ],
        [
            jax.ShapeDtypeStruct((feats, 2 * tokens), BF16),
            jax.ShapeDtypeStruct((2 * tokens, feats // 2), BF16),
        ],
        2.0,
        "all_tokens",
        place,
        (both, far, both, far),
        gate,
    )


def add_end(place, own, got, gate, passed):
    _, tokens, width = own.shape

    def kernel(place_ref, own_ref, got_ref, *refs):
        sum_ref, low_ref = refs[len(passed) : len(passed) + 2]
        total = own_ref[...] + got_ref[...].astype(F32)
        sum_ref[...] = total
        low_ref[...] = total.astype(BF16)

    block = pl.BlockSpec((2, tokens, width), lambda g, place: (g, 0, 0))
    return call(
        kernel,
        (2,),
        [block, block] + [ANY] * len(passed),
        [block, block] + [ANY] * len(passed),
        [jax.ShapeDtypeStruct(own.shape, F32), jax.ShapeDtypeStruct(own.shape, BF16)]
        + [jax.ShapeDtypeStruct(p.shape, p.dtype) for p in passed],
        0.75,
        "add_end",
        place,
        (own, got, *passed),
        gate,
        {3 + i: 2 + i for i in range(len(passed))},
    )


def activate(place, total, got, gate):
    _, tokens, width = total.shape

    def kernel(place_ref, total_ref, got_ref, made_ref):
        g = pl.program_id(0)
        act_full, gelu_slope = gelu_parts(total_ref[1 - g] + got_ref[1 - g].astype(F32))
        made_ref[1 - g] = act_full.astype(BF16)
        made_ref[g] = ((total_ref[g] + got_ref[g].astype(F32)) * gelu_slope).astype(BF16)

    block = pl.BlockSpec((2, tokens, width), lambda g, place: (g, 0, 0))
    return call(
        kernel,
        (2,),
        [block, block],
        block,
        jax.ShapeDtypeStruct(total.shape, BF16),
        1.1,
        "activate",
        place,
        (total, got),
        gate,
    )


def choose(place, made, got, gate):
    count = len(made)
    _, tokens, width = made[0].shape

    def kernel(place_ref, *refs):
        for i in range(count):

            @pl.when(place_ref[1] == 0)
            def _():
                refs[-2][i] = refs[i][0]
                refs[-1][3 * i : 3 * i + 3] = refs[i][1:]

            @pl.when(place_ref[1] != 0)
            def _():
                refs[-2][i] = refs[count + i][0]
                refs[-1][3 * i : 3 * i + 3] = refs[count + i][1:]

    whole = pl.BlockSpec((4, tokens, width), lambda g, place: (0, 0, 0))
    shapes = [(count, tokens, width), (3 * count, tokens, width)]
    return call(
        kernel,
        (1,),
        [whole] * (2 * count),
        [pl.BlockSpec(shape, lambda g, place: (0, 0, 0)) for shape in shapes],
        [jax.ShapeDtypeStruct(shape, BF16) for shape in shapes],
        0.6,
        "choose",
        place,
        (*made, *got),
        gate,
    )


def gradients(place, first, three, far, w_in, xt, s_half, acc, totals, gate, start, count, width):
    tokens = first.shape[1]
    feats, hidden = w_in.shape
    rows = tokens // 2
    with_input, with_weights = acc is not None, far is not None
    fresh_input, fresh_weights = with_input and not acc, with_weights and not totals

    def kernel(place_ref, first_ref, three_ref, *refs):
        refs = list(refs)
        step = pl.program_id(0)
        g = step % 2
        if with_weights:
            far_ref, xt_ref, s_ref = refs[:3]
            del refs[:3]
        if with_input:
            w_ref, sems, buf = refs.pop(0), refs.pop(), refs.pop()
            if not fresh_input:
                acc_refs = refs[:2]
                del refs[:2]

            def copy(i):
                at = half_offset(place_ref, i % 2 == 0, hidden, start + i // 2 * width)
                return pltpu.make_async_copy(w_ref.at[:, pl.ds(at, width)], buf.at[i], sems.at[i])

            @pl.when(step == 0)
            def _():
                for i in range(2 * count):
                    copy(i).start()

        if with_weights and not fresh_weights:
            del refs[:2]
        if with_weights:
            in_ref, out_ref = refs[-2:]
            pg = jnp.concatenate([first_ref[0], far_ref[2]], axis=0)
            in_ref[...] = dot(xt_ref[...], pg, 1, 0)
            act = jnp.concatenate([three_ref[g], far_ref[1 - g]], axis=0)
            out_ref[...] = dot(act, s_ref[...], 0, 0)
        if with_input:
            for i in range(2 * count):

                @pl.when(step == i)
                def _():
                    copy(i).wait()
                    part = dot(three_ref[2] if i % 2 else first_ref[0], buf[i], 1, 1)
                    for k in range(2):
                        mine = part[k * rows : (k + 1) * rows]
                        if i == 0:
                            refs[k][...] = mine if fresh_input else acc_refs[k][...] + mine
                        else:
                            refs[k][...] += mine

    blocks = lambda n: pl.BlockSpec((n, tokens, width), lambda step, place: (step // 2, 0, 0))
    whole = pl.BlockSpec((rows, feats), lambda step, place: (0, 0))
    args, in_specs = [first, three], [blocks(1), blocks(3)]
    out_specs, out_shape, aliases, scratch = [], [], {}, []
    if with_weights:
        args += [far, xt, s_half]
        in_specs += [
            blocks(3),
            pl.BlockSpec((feats // 2, 2 * tokens), lambda step, place: (step % 2, 0)),
            pl.BlockSpec((2 * tokens, feats // 2), lambda step, place: (0, 0)),
        ]
    if with_input:
        args += [w_in, *acc]
        in_specs += [HBM] + [whole] * len(acc)
        out_specs += [whole] * 2
        out_shape += [jax.ShapeDtypeStruct((rows, feats), F32)] * 2
        scratch = [
            pltpu.VMEM((2 * count, feats, width), BF16),
            pltpu.SemaphoreType.DMA((2 * count,)),
        ]
    if with_weights:
        per_half, first_chunk = hidden // 2 // width, start // width

        def out_place(step, place):
            half = jnp.where(step % 2 == 0, place[0], 1 - place[0])
            return half * per_half + first_chunk + step // 2, 0

        for total in totals:
            aliases[1 + len(args)] = len(out_shape) + len(aliases)
            args += [in_hbm(total)]
            in_specs += [HBM]
        out_specs += [
            pl.BlockSpec((feats // 2, width), lambda step, place: (step % 2, first_chunk + step // 2)),
            pl.BlockSpec((width, feats // 2), out_place),
        ]
        out_shape += [pltpu.HBM((feats, hidden // 2), F32), pltpu.HBM((hidden, feats // 2), F32)]
    outs = call(
        kernel,
        (2 * count,),
        in_specs,
        out_specs,
        out_shape,
        5.8 if with_input and with_weights else 20.0,
        "gradients",
        place,
        args,
        gate,
        aliases,
        scratch,
    )
    return (tuple(outs[:2]) if with_input else None), (tuple(outs[-2:]) if with_weights else totals)


def plan(units):
    tail = TAIL * TAILS
    main = units - tail
    if main > 0 and main % MAIN == 0 and main % TAIL == 0 and units % MAIN == 0 and units % TAIL == 0:
        widths = [MAIN] * (main // MAIN) + [TAIL] * TAILS
    else:
        count = max(k for k in range(1, CHUNKS + 1) if units % k == 0)
        widths = [units // count] * count
    return [(128 * sum(widths[:i]), 128 * width) for i, width in enumerate(widths)]


def doubling_gather(value, axis, size):
    bit = size // 2
    while bit:
        got = lax.ppermute(value, axis, [(i, i ^ bit) for i in range(size)])
        value = jnp.concatenate([value, got], axis=1)
        bit //= 2
    return value


def halving_sum(keep, send, axis, size):
    bit = 1
    while True:
        got = lax.ppermute(send, axis, [(i, i ^ bit) for i in range(size)])
        bit *= 2
        if bit == size:
            return keep + got.astype(F32)
        rows = keep.shape[0] // 2
        send = (keep[rows:] + got[rows:].astype(F32)).astype(BF16)
        keep = keep[:rows] + got[:rows].astype(F32)


def per_device(sizes, layer_input, w_in, w_out, out_grad, drop_seed, drop_step):
    rows, cols, depths = sizes
    row, col, depth = lax.axis_index("row"), lax.axis_index("col"), lax.axis_index("depth")
    own_tokens, feats = layer_input.shape
    hidden = w_in.shape[1]
    assert rows == 4 and depths == 2 and hidden % 256 == 0
    chunks = plan(hidden // 256)
    w_in, w_out = in_hbm(w_in), in_hbm(w_out)
    swap = [(0, 1), (1, 0)]
    is_end = (row == 0) | (row == 3)
    place = jnp.stack([depth, is_end]).astype(jnp.int32)
    inward, outward, across = [(0, 1), (3, 2)], [(1, 0), (2, 3)], [(1, 2), (2, 1)]

    keep_flags = keep_mask(
        drop_seed, drop_step, (depth * cols + col) * own_tokens, row * feats, own_tokens, feats, D
    )
    own_scaled = jnp.where(
        keep_flags, out_grad.astype(F32) * keep_scale, jnp.zeros((), F32)
    ).astype(BF16)
    both = doubling_gather(jnp.stack([layer_input, own_scaled]), "col", cols)
    both_far = lax.ppermute(both, "depth", swap)

    own, low, total, made, got, first, three, far = ({} for _ in range(8))
    acc, totals = (), ()
    last = ()
    n = len(chunks)
    to_prepare, c = [], 0
    while c < n:
        count = 2 if c >= 2 and c + 1 < n and chunks[c][1] == chunks[c + 1][1] else 1
        to_prepare.append((c, count))
        c += count
    to_prepare[1:3] = to_prepare[2:0:-1]

    def prepare():
        nonlocal last
        if to_prepare:
            start, count = to_prepare.pop(0)
            sums = partial_sums(place, both, w_in, w_out, last, chunks[start][0], count, chunks[start][1])
            for i in range(count):
                own[start + i], low[start + i] = sums[2 * i], sums[2 * i + 1]
            last = (sums[-1],)

    def finish(c, acc, totals, part=None):
        return gradients(
            place, first[c], three[c], None if part == "input" else far[c], w_in, xt, s_half,
            None if part == "weights" else acc, totals, last, chunks[c][0], 1, chunks[c][1],
        )

    prepare()
    prepare()
    prepare()
    todo = []
    for c in range(n + 2):
        if c < n:
            got_end = lax.ppermute(low[c], "row", inward)
            while to_prepare and c + 2 < n and c + 2 not in low:
                prepare()
            passed = (low[c + 2],) if c + 2 < n else ()
            total[c], low[c], *passed = add_end(place, own[c], got_end, last, passed)
            if passed:
                (low[c + 2],) = passed
            last = (low[c],)
        if 1 <= c <= n:
            got_across = lax.ppermute(low[c - 1], "row", across)
            made[c - 1] = activate(place, total[c - 1], got_across, last)
            last = (made[c - 1],)
        if c >= 2:
            got[c - 2] = lax.ppermute(made[c - 2], "row", outward)
            first[c - 2], three[c - 2] = choose(place, [made[c - 2]], [got[c - 2]], last)
            far[c - 2] = lax.ppermute(three[c - 2], "depth", swap)
            todo.append(c - 2)
            last = (first[c - 2],)
        prepare()
        if c == 1:
            xt, s_half = all_tokens(place, both, both_far, last)
            last = (s_half,)
        if len(todo) > 1 and c < n + 1:
            acc, totals = finish(todo.pop(0), acc, totals)
            last = (acc[1],)
        if c == n:
            acc, _ = finish(todo[0], acc, (), "input")
            last = (acc[1],)
        if c == n + 1:
            acc, _ = finish(todo[1], acc, (), "input")
            last = (acc[1],)
    for c in todo:
        _, totals = finish(c, None, totals, "weights")
        last = ()
    input_grad = halving_sum(*acc, "col", cols)
    return (input_grad, totals[0], totals[1])


def solution(mesh):
    placed = (
        P(("depth", "col"), "row"),
        P("row", "col"),
        P("col", "row"),
        P(("depth", "col"), "row"),
        P(),
        P(),
    )
    sizes = tuple(mesh.shape[name] for name in ("row", "col", "depth"))
    return jax.shard_map(
        functools.partial(per_device, sizes),
        mesh=mesh,
        in_specs=placed,
        out_specs=(
            P(("depth", "col"), "row"),
            P("row", ("col", "depth")),
            P("col", ("row", "depth")),
        ),
        check_vma=False,
    )
```
